128 devices in a mesh: slab: 16 (over z, x), cross: 8 (over y, core).
Axes of the slice: x: 4, y: 4, z: 4, core: 2. Of those that a mesh axis runs over, the one named last changes fastest.
Arguments:
- fields: bfloat16 [256, 64, 257, 128], P('slab', 'cross'), may hold values from -1.5 to 1.5
- strain_map: bfloat16 [162, 108], replicated, may hold values from -0.625 to 0.625
- quad_weight: float32 [27, 524288], P(None, ('slab', 'cross')), may hold values from 0.25 to 4
- param: float32 [1048576], P(('slab', 'cross')), may hold values from -3 to 3
- elem_order: int32 [524288], P(('slab', 'cross')), may hold values from 0 to 4095, as said below
- send_elem: int32 [128, 128, 64], P(('slab', 'cross')), may hold values from 0 to 4095, as said below
- send_count: int32 [128, 128], P(('slab', 'cross')), may hold values from 0 to 64, as said below
- recv_cell: int32 [128, 128, 64], P(('slab', 'cross')), may hold values from 0 to 8191
Outputs:
- hessian_terms: float32 [16, 8, 1048576], P(None, None, ('slab', 'cross'))
The draws below stay inside these ranges and needn't reach their ends.
Inputs may be any that keep to these rules, and one draw needn't show every extreme that they name: `elem_order`: each device's 4096 entries are a permutation of its local element positions. `send_elem`: the live slots of one sender, over all owners, name each of its 4096 elements exactly once; slots at or past a block's count hold arbitrary element numbers. `send_count`: each sender's counts sum to 4096; one owner gets 64 live slots from every sender. `recv_cell`: slots at or past the sender's count carry nothing.
All inputs are finite; a program needn't handle non-finite values.
Results may differ from the reference program's by a relative error of at most 0.0003.
Values may be sent and summed in bfloat16 or wider, within the bound.
No kernel may reach another device: no remote copies, remote signals or barrier semaphores. Data moves between devices by JAX's collectives and lax.ppermute only.
A program may use at most 128 MiB of HBM per device.

```python
import math
import jax
import jax.numpy as jnp
from jax import lax

EX = 8
EY = 4
EZ = 128
PC_DEV = 8192
DIRS = 16
CORNERS = 8
STRAIN_ROWS = 162
EL_DEV = 4096
OWNERS = 128
CAP = 64
NXN = 256
NYN = 64
NZN = 257
ELEMS = 524288
CELLS = 1048576
N_CROSS = 8


def draw_elem_order(key, part):
    keys = jax.random.split(key, OWNERS)
    perms = jax.vmap(lambda one_key: jax.random.permutation(one_key, EL_DEV))(keys)
    return perms.reshape(-1).astype(jnp.int32)


def routing_tables(key):
    base = jax.random.fold_in(key, 11)
    key_hot, key_len, key_elem = jax.random.split(base, 3)
    hot_owner = jax.random.randint(key_hot, (), 0, OWNERS)
    sender = jnp.arange(OWNERS, dtype=jnp.int32)[:, None]
    rank = jnp.arange(OWNERS, dtype=jnp.int32)[None, :]
    owner_at = (sender + rank) % OWNERS
    run_len = jax.random.randint(key_len, (OWNERS, OWNERS), CAP // 2, CAP + 1)
    run_len = jnp.where(owner_at == hot_owner, 0, run_len)
    ends = CAP + jnp.cumsum(run_len, axis=1)
    starts = ends - run_len
    count_rank = jnp.clip(ends, 0, EL_DEV) - jnp.clip(starts, 0, EL_DEV)
    start_rank = jnp.clip(starts, 0, EL_DEV)
    rank_of = (rank - sender) % OWNERS
    counts = jnp.take_along_axis(count_rank, rank_of, axis=1)
    offsets = jnp.take_along_axis(start_rank, rank_of, axis=1)
    counts = jnp.where(rank == hot_owner, CAP, counts)
    offsets = jnp.where(rank == hot_owner, 0, offsets)
    keys = jax.random.split(key_elem, OWNERS)
    perms = jax.vmap(lambda one_key: jax.random.permutation(one_key, EL_DEV))(keys)
    positions = jnp.minimum(offsets[:, :, None] + jnp.arange(CAP, dtype=jnp.int32)[None, None, :], EL_DEV - 1)
    elements = perms[jnp.arange(OWNERS, dtype=jnp.int32)[:, None, None], positions]
    return (elements.astype(jnp.int32), counts.astype(jnp.int32))


def draw_send_elem(key, part):
    elements, counts = routing_tables(key)
    return elements


def draw_send_count(key, part):
    elements, counts = routing_tables(key)
    return counts


def with_ends(values, rng, smallest, top_value):
    longest = values.shape.index(max(values.shape))
    spots = []
    for shift in (0, 1):
        where = [jax.random.randint(jax.random.fold_in(rng, axis), (), 0, length) for axis, length in enumerate(values.shape)]
        where[longest] = (where[longest] + shift) % values.shape[longest]
        spots.append(tuple(where))
    return values.at[spots[0]].set(smallest).at[spots[1]].set(top_value)


def shard_levels(key, shape, pieces, smallest, largest):
    gain, own = 1.0, jax.random.fold_in(key, 6)
    for axis_at, blocks in pieces:
        heights = jnp.exp(jax.random.uniform(jax.random.fold_in(own, axis_at), (blocks,), jnp.float32, smallest / len(pieces), largest / len(pieces)))
        gain = gain * jnp.repeat(heights, shape[axis_at] // blocks).reshape([-1 if axis == axis_at else 1 for axis in range(len(shape))])
    return gain


def noise(key, extent, scale, reach, pieces=(), kind=jnp.bfloat16):
    entries = jax.random.normal(key, extent, jnp.float32) * scale
    if len(pieces) > 0:
        entries = shard_levels(key, extent, pieces, -0.22, 0.18) * entries
    return jnp.clip(entries, min=-reach, max=reach).astype(kind)


def setup_inputs(seed: int = 0) -> dict:
    key_list = jax.random.split(jax.random.key(seed), 9)
    return {
        "fields": noise(key_list[0], (NXN, NYN, NZN, 128), 0.25, 1.5, ((0, 16), (1, 8))),
        "strain_map": noise(key_list[1], (STRAIN_ROWS, 108), 108 ** -0.5, 0.625),
        "quad_weight": jnp.clip(jnp.exp(math.log(4.0) - 2.7725887 * jax.random.uniform(key_list[2], (27, ELEMS), jnp.float32) ** shard_levels(key_list[2], (27, ELEMS), ((1, 128),), -0.2, 0.2)), 0.25, 4.0),
        "param": noise(key_list[3], (CELLS,), 0.5, 3.0, ((0, 128),), jnp.float32),
        "elem_order": draw_elem_order(jax.random.fold_in(key_list[8], 71), 0),
        "send_elem": draw_send_elem(jax.random.fold_in(key_list[8], 71), 0),
        "send_count": draw_send_count(jax.random.fold_in(key_list[8], 71), 0),
        "recv_cell": with_ends(jax.random.randint(key_list[7], (OWNERS, OWNERS, CAP), 0, PC_DEV), jax.random.fold_in(key_list[7], 1), 0, PC_DEV - 1).astype(jnp.int32),
    }


def gauss_basis():
    spread = math.sqrt(0.15)
    places = jnp.array([0.5 - spread, 0.5, 0.5 + spread], jnp.float32)
    points = jnp.arange(27, dtype=jnp.int32)
    coeffs = jnp.arange(8, dtype=jnp.int32)
    result = jnp.ones((27, 8), jnp.float32)
    for point_axis, coeff_axis in ((points // 9, coeffs // 4), (points // 3 % 3, coeffs // 2 % 2), (points % 3, coeffs % 2)):
        where_x = places[point_axis][:, None]
        result = result * jnp.where(coeff_axis[None, :] == 1, where_x, 1.0 - where_x)
    return result

def element_partials(node_rows, numbering, weights, strain_map, y_elems, z_elems):
    z_nodes = 2 * z_elems + 1
    y_nodes = 2 * y_elems + 1
    x_elem = numbering // (y_elems * z_elems)
    y_elem = numbering // z_elems % y_elems
    z_elem = numbering % z_elems
    first_node = (2 * x_elem * y_nodes + 2 * y_elem) * z_nodes + 2 * z_elem
    corner = jnp.arange(27, dtype=jnp.int32)
    offsets = (corner // 9 * y_nodes + corner // 3 % 3) * z_nodes + corner % 3
    elem_count = numbering.shape[0]
    block_len = min(512, elem_count)
    strain_table = strain_map.reshape(strain_map.shape[0], 27, 4).astype(jnp.float32)
    basis = gauss_basis()

    def one_block(block_index):
        first_row = block_index * block_len
        node_ids = lax.dynamic_slice_in_dim(first_node, first_row, block_len)
        node_values = node_rows[node_ids[:, None] + offsets[None, :]]
        shaped = node_values.reshape(block_len, 27, 2, 4, -1).astype(jnp.float32)
        strain = jnp.einsum('enfcd,qnc->fedq', shaped, strain_table, precision=lax.Precision.HIGHEST)
        product = strain[0] * strain[1]
        product = lax.optimization_barrier(jnp.sum(product.reshape(block_len, product.shape[1], 27, 6), axis=-1))
        block_weight = lax.dynamic_slice_in_dim(weights, first_row, block_len, 1)
        weighted = product * block_weight.T[:, None, :]
        return jnp.einsum('edg,gt->edt', weighted, basis, precision=lax.Precision.HIGHEST)
    per_block = lax.map(one_block, jnp.arange(elem_count // block_len, dtype=jnp.int32))
    return per_block.reshape(elem_count, -1)

def reference(fields, strain_map, quad_weight, param, elem_order, send_elem, send_count, recv_cell):
    extended = jnp.pad(fields, ((0, 1), (0, 1), (0, 0), (0, 0)))
    z_nodes = extended.shape[2]
    channels = extended.shape[3]
    zero = jnp.zeros((), jnp.int32)
    slot_ids = jnp.arange(CAP, dtype=jnp.int32)
    owner_ids = jnp.arange(OWNERS, dtype=jnp.int32)
    lanes = DIRS * CORNERS

    def add_sender(gradient, sender):
        slab_pos = sender // N_CROSS
        cross_pos = sender % N_CROSS
        piece = lax.dynamic_slice(extended, (slab_pos * (2 * EX), cross_pos * (2 * EY), zero, zero), (2 * EX + 1, 2 * EY + 1, z_nodes, channels))
        node_rows = piece.reshape(-1, channels)
        numbering = lax.dynamic_slice_in_dim(elem_order, sender * EL_DEV, EL_DEV)
        weights = lax.dynamic_slice_in_dim(quad_weight, sender * EL_DEV, EL_DEV, 1)
        partial_value = element_partials(node_rows, numbering, weights, strain_map, EY, EZ)
        values = partial_value[send_elem[sender]]
        live_slots = slot_ids[None, :] < send_count[sender][:, None]
        values = jnp.where(live_slots[:, :, None], values, 0.0)
        cell_ids = owner_ids[:, None] * PC_DEV + recv_cell[:, sender, :]
        gradient = gradient.at[cell_ids.reshape(-1)].add(values.reshape(-1, lanes))
        return (gradient, None)
    gradient, unused = lax.scan(add_sender, jnp.zeros((CELLS, lanes), jnp.float32), jnp.arange(OWNERS, dtype=jnp.int32))
    terms = gradient.T.reshape(DIRS, CORNERS, CELLS)
    return terms * jnp.exp(param)[None, None, :]
```

```python
import functools

import jax
import jax.numpy as jnp
import numpy as np
from jax import lax
from jax.experimental import pallas as pl
from jax.experimental.pallas import tpu as pltpu
from jax.sharding import PartitionSpec as P

AXES = ("slab", "cross")
F32, BF16, I32 = jnp.float32, jnp.bfloat16, jnp.int32
VMEM_BYTES = 56 * 1024 * 1024
ROWS_Q = 168
ROWS_K = 48


def shifted(value, axis):
    count = lax.axis_size(axis)
    return lax.ppermute(value, axis, [(source, source - 1) for source in range(1, count)])


def shifted_both(value):
    slabs, crosses = lax.axis_size("slab"), lax.axis_size("cross")
    pairs = [
        (u * crosses + v, (u - 1) * crosses + v - 1)
        for u in range(1, slabs)
        for v in range(1, crosses)
    ]
    return lax.ppermute(value, AXES, pairs)


def gauss_basis():
    spread = np.sqrt(0.15)
    places = np.array([0.5 - spread, 0.5, 0.5 + spread], np.float32)
    one = np.stack([np.float32(1.0) - places, places], 1).astype(np.float64)
    return np.einsum("ai,bj,ck->abcijk", one, one, one).reshape(27, 8)


def tables():
    q_rows = np.zeros((ROWS_Q, 162), np.float32)
    for m in range(6):
        for g in range(24):
            q_rows[m * 24 + g, 6 * g + m] = 1
        for g in range(3):
            q_rows[144 + (m // 2) * 8 + (m % 2) * 3 + g, 6 * (24 + g) + m] = 1
    cols = np.zeros((108, 3 * ROWS_K), np.float32)
    places = [(0, 0), (0, 1), (1, 0), (1, 1), (2, 0), (2, 1), (0, 2), (1, 2), (2, 2)]
    for i in range(3):
        for place, (j, k) in enumerate(places):
            for c in range(4):
                cols[4 * (9 * i + 3 * j + k) + c, ROWS_K * i + 4 * place + c] = 1
    perm = np.zeros((256, 256), np.float32)
    for f in range(2):
        for d in range(16):
            for s in range(2):
                for c in range(4):
                    perm[(f * 16 + d) * 8 + s * 4 + c, s * 128 + f * 64 + c * 16 + d] = 1
    basis = gauss_basis()
    rows = np.concatenate([basis[:27], basis[24:27], np.zeros((2, 8))], 0).T
    high = rows.astype(np.float32).astype(jnp.bfloat16)
    low = (rows - high.astype(np.float64)).astype(np.float32).astype(jnp.bfloat16)
    eye = np.eye(16)
    block = lambda x: np.einsum("ab,tg->agbt", eye, x.astype(np.float64)).reshape(512, 128)
    split = np.concatenate([block(high), block(low)], 1)
    bf = lambda x: x.astype(jnp.bfloat16)
    return bf(q_rows), bf(cols), bf(perm), bf(split)


def dot(a, b, dims=((1,), (0,))):
    return lax.dot_general(a, b, (dims, ((), ())), preferred_element_type=F32)


def prepare_kernel(order_s, weight, order_v, send, count, placed, slots, turned, spread):
    blocks = weight.shape[1] // 128

    def turn(blk, _):
        at = pl.ds(pl.multiple_of(blk * 128, 128), 128)
        w = weight[:, at]
        rows = jnp.concatenate([w, w[24:27], jnp.zeros((2, 128), F32)], 0)
        turned[at, :] = rows.T
        return 0

    lax.fori_loop(0, blocks, turn, 0)

    def place(step, _):
        for r in range(16):
            e = step * 16 + r
            spread[pl.ds(order_s[e], 1), :] = turned[pl.ds(e, 1), :]
        return 0

    lax.fori_loop(0, blocks * 8, place, 0)

    def back(blk, _):
        at = pl.ds(pl.multiple_of(blk * 128, 128), 128)
        placed[blk] = spread[at, :].T
        return 0

    lax.fori_loop(0, blocks, back, 0)
    live = lax.broadcasted_iota(I32, send.shape, 0) < count[...]
    for part in range(send.shape[0] // 8):
        at = slice(part * 8, part * 8 + 8)
        asked = send[at, :]
        low, high = asked & 127, asked >> 7
        found = jnp.zeros(asked.shape, I32)
        for row in range(blocks):
            table = jnp.broadcast_to(order_v[row : row + 1, :], asked.shape)
            found = jnp.where(high == row, jnp.take_along_axis(table, low, axis=1), found)
        slots[at, :] = jnp.where(live[at, :], found, weight.shape[1])


def partial_kernel(
    slots, odd, even, side_odd, side_even, face, corner, weight, smap, qrow, kcol, perm, basis,
    words, flat, flat_side, taps, mapped, top_part, low_part, rows, low_code, high_code,
):
    step = pl.program_id(0)
    last = pl.num_programs(0) - 1
    elem_rows = 4

    @pl.when(step == 0)
    def _():
        wide = dot(qrow[...], smap[...]).astype(BF16)
        mapped[...] = dot(wide, kcol[...]).astype(BF16)

    def fill(where, plane, side):
        flat[where, 0 : 257 * 8, :] = plane.astype(F32).reshape(257 * 8, 128)
        flat_side[where, 0:257, :] = side.astype(F32)

    def turn(where, slot):
        def line(y, k):
            if y < 8:
                return flat[where, pl.ds(8 * k + y, 128, stride=16), :].astype(BF16)
            return flat_side[where, pl.ds(k, 128, stride=2), :].astype(BF16)

        def ordered(one, other):
            pair = jnp.concatenate([jnp.concatenate(one, 1), jnp.concatenate(other, 1)], 0)
            both = dot(perm[...], pair, ((1,), (1,)))
            return both[:, :128].reshape(32, 8, 128), both[:, 128:].reshape(32, 8, 128)

        def near(y):
            return line(y, 0), line(y, 1)

        def far(y):
            return line(y, 2), line(min(y + 1, 8), 2)

        before, beyond = ordered(near(0), far(0))
        for b in range(elem_rows):
            y = 2 * b
            held = beyond
            middle, after = ordered(near(y + 1), near(y + 2))
            if b % 2 == 0:
                beyond, later = ordered(far(y + 2), far(y + 4))
            else:
                beyond = later
            at = b * ROWS_K
            taps[slot, :, at : at + 16, :] = jnp.concatenate([before, middle], 1).astype(BF16)
            taps[slot, :, at + 16 : at + 32, :] = jnp.concatenate([after, held], 1).astype(BF16)
            taps[slot, :, at + 32 : at + 48, :] = jnp.concatenate([beyond, beyond], 1).astype(BF16)
            before = after

    @pl.when(step > 0)
    def _():
        fill(0, odd[0], side_odd[0])
        turn(0, lax.rem(2 * step + 2, 3))

    @pl.when(step < last)
    def _():
        fill(1, even[0], side_even[0])

    @pl.when(step == last)
    def _():
        fill(1, face[...], corner[...])

    turn(1, lax.rem(2 * step, 3))

    @pl.when(step > 0)
    def _():
        a = step - 1
        plane_slots = [lax.rem(2 * a + i, 3) for i in range(3)]

        def element_row(b, _):
            at = pl.ds(pl.multiple_of(b * ROWS_K, 16), ROWS_K)
            scale = weight[a * elem_rows + b]
            pieces = []
            for d in range(16):
                parts = [
                    jnp.concatenate([taps[s, d, at, :], taps[s, 16 + d, at, :]], 1)
                    for s in plane_slots
                ]
                strain = dot(mapped[...], jnp.concatenate(parts, 0))
                product = strain[:, :128] * strain[:, 128:]
                main = product[0:24]
                for m in range(1, 6):
                    main = main + product[24 * m : 24 * m + 24]
                rest = product[144:152] + product[152:160] + product[160:168]
                summed = jnp.concatenate([main, rest], 0) * scale
                pieces.append(summed)
                if d % 4 == 3:
                    by_elem = jnp.concatenate(pieces, 0).T
                    pieces = []
                    high = by_elem.astype(BF16)
                    to = pl.ds(pl.multiple_of(b * 128, 128), 128)
                    top_part[to, (d - 3) * 32 : (d + 1) * 32] = high
                    low_part[to, (d - 3) * 32 : (d + 1) * 32] = (by_elem - high.astype(F32)).astype(BF16)
            return 0

        lax.fori_loop(0, elem_rows, element_row, 0, unroll=2)
        out_at = pl.ds(pl.multiple_of(a * elem_rows * 128, 128), elem_rows * 128)
        both = dot(top_part[...], basis[...])
        rows[out_at, :] = both[:, :128] + (both[:, 128:] + dot(low_part[...], basis[:, :128]))

    @pl.when(step == last)
    def _():
        count = rows.shape[0]
        chunk = 128

        def largest(i, top):
            block = rows[pl.ds(pl.multiple_of(i * chunk, chunk), chunk), :]
            return jnp.maximum(top, jnp.max(jnp.abs(block).reshape(chunk // 8, 8, 128), 0))

        top = lax.fori_loop(0, count // chunk, largest, jnp.full((8, 128), 1e-30, F32))
        top = jnp.max(jnp.max(top, axis=1, keepdims=True), axis=0, keepdims=True)
        level = jnp.ceil(jnp.log2(jnp.broadcast_to(top, (1, 128))) * 4096.0 + 1.0)
        inverse = jnp.exp2(level * (-1.0 / 4096.0))

        def encode(i, _):
            at = pl.ds(pl.multiple_of(i * chunk, chunk), chunk)
            block = rows[at, :]
            size = jnp.maximum(jnp.abs(block) * inverse, 1e-36)
            root = jnp.exp2(jnp.log2(size) * (1.0 / 3.0)) * 32767.0
            code = jnp.minimum(root + 0.5, 32767.0).astype(I32)
            code = jnp.where(block < 0.0, -code, code)
            low_code[at, :] = code & 65535
            high_code[at, :] = code << 16
            return 0

        lax.fori_loop(0, count // chunk, encode, 0)
        low_code[count : count + 8, :] = jnp.zeros((8, 128), I32)
        high_code[count : count + 8, :] = jnp.zeros((8, 128), I32)

        def gather(o, _):
            for j in range(32):
                first = low_code[pl.ds(slots[j, o], 1), :]
                second = high_code[pl.ds(slots[32 + j, o], 1), :]
                words[o, j] = first | second
            words[o, 32] = level.astype(I32)
            return 0

        lax.fori_loop(0, words.shape[0], gather, 0)


def collect_kernel(cells, words, param, out, *sums):
    count = out.shape[1]

    def clear(i, _):
        for total in sums:
            total[pl.ds(pl.multiple_of(i * 128, 128), 128), :] = jnp.zeros((128, 128), F32)
        return 0

    lax.fori_loop(0, count // 128, clear, 0)

    def add(p, _):
        scale = jnp.exp2(words[p, 32].astype(F32) * (1.0 / 4096.0)) * (1.0 / 32767.0**3)
        for j in range(0, 32, 2):
            ats, values = [], []
            for step in (j, j + 1):
                word = words[p, step]
                for half, where in ((lax.shift_right_arithmetic(word << 16, 16), step),
                                    (lax.shift_right_arithmetic(word, 16), step + 32)):
                    code = half.astype(F32)
                    values.append(code * code * (code * scale))
                    ats.append(pl.ds(cells[where, p], 1))
            held = [total[at, :] for total, at in zip(sums, ats)]
            for total, at, was, value in zip(sums, ats, held, values):
                total[at, :] = was + value
        return 0

    lax.fori_loop(0, words.shape[0], add, 0)

    def finish(i, _):
        at = pl.ds(pl.multiple_of(i * 128, 128), 128)
        total = (sums[0][at, :] + sums[1][at, :]) + (sums[2][at, :] + sums[3][at, :])
        out[:, at] = total.T * jnp.exp(param[pl.ds(i, 1), :])
        return 0

    lax.fori_loop(0, count // 128, finish, 0, unroll=4)


def whole(shape):
    zeros = (0,) * len(shape)
    return pl.BlockSpec(shape, lambda *_: zeros)


def on_device(fields, strain_map, quad_weight, param, elem_order, send_elem, send_count, recv_cell):
    planes = jnp.transpose(fields, (0, 2, 1, 3))
    face = jnp.transpose(shifted(fields[0:1], "slab"), (0, 2, 1, 3))[0]
    side = shifted(fields[:, 0:1], "cross")[:, 0]
    corner = shifted_both(fields[0:1, 0:1])[0, 0]
    q_rows, k_cols, perm, basis = tables()
    elems = elem_order.shape[0]
    smem = pl.BlockSpec(memory_space=pltpu.SMEM)
    vmem = pl.BlockSpec(memory_space=pltpu.VMEM)
    params = pltpu.CompilerParams(vmem_limit_bytes=VMEM_BYTES)

    placed, slots = pl.pallas_call(
        prepare_kernel,
        out_shape=(
            jax.ShapeDtypeStruct((elems // 128, 32, 128), F32),
            jax.ShapeDtypeStruct((64, 128), I32),
        ),
        in_specs=[smem] + [vmem] * 4,
        out_specs=(vmem, vmem),
        scratch_shapes=[pltpu.VMEM((elems, 32), F32), pltpu.VMEM((elems, 32), F32)],
        compiler_params=params,
    )(elem_order, quad_weight, elem_order.reshape(elems // 128, 128), send_elem[0].T, send_count)

    block = (1, 257, 8, 128)
    side_block = (1, 257, 128)
    odd = lambda s: jnp.maximum(2 * s - 1, 1)
    even = lambda s: jnp.minimum(2 * s, 14)
    words = pl.pallas_call(
        partial_kernel,
        grid=(9,),
        out_shape=jax.ShapeDtypeStruct((128, 33, 1, 128), I32),
        in_specs=[
            smem,
            pl.BlockSpec(block, lambda s: (odd(s), 0, 0, 0)),
            pl.BlockSpec(block, lambda s: (even(s), 0, 0, 0)),
            pl.BlockSpec(side_block, lambda s: (odd(s), 0, 0)),
            pl.BlockSpec(side_block, lambda s: (even(s), 0, 0)),
            whole((257, 8, 128)),
            whole((257, 128)),
            whole(placed.shape),
            whole(strain_map.shape),
            whole(q_rows.shape),
            whole(k_cols.shape),
            whole(perm.shape),
            whole(basis.shape),
        ],
        out_specs=whole((128, 33, 1, 128)),
        scratch_shapes=[
            pltpu.VMEM((2, 2080, 128), F32),
            pltpu.VMEM((2, 264, 128), F32),
            pltpu.VMEM((3, 32, 4 * ROWS_K, 128), BF16),
            pltpu.VMEM((ROWS_Q, 3 * ROWS_K), BF16),
            pltpu.VMEM((512, 512), BF16),
            pltpu.VMEM((512, 512), BF16),
            pltpu.VMEM((elems, 128), F32),
            pltpu.VMEM((elems + 8, 128), I32),
            pltpu.VMEM((elems + 8, 128), I32),
        ],
        compiler_params=params,
    )(slots, planes, planes, side, side, face, corner, placed, strain_map, q_rows, k_cols, perm, basis)

    arrived = lax.all_to_all(words, AXES, split_axis=0, concat_axis=0, tiled=True)
    cells = param.shape[0]
    terms = pl.pallas_call(
        collect_kernel,
        out_shape=jax.ShapeDtypeStruct((128, cells), F32),
        in_specs=[smem, vmem, vmem],
        out_specs=vmem,
        scratch_shapes=[pltpu.VMEM((cells, 128), F32)] * 4,
        compiler_params=params,
    )(recv_cell[0].T, arrived, param.reshape(cells // 128, 128))
    return terms.reshape(16, 8, cells)


def solution(mesh):
    return jax.shard_map(
        on_device,
        mesh=mesh,
        in_specs=(
            P("slab", "cross", None, None),
            P(),
            P(None, AXES),
            P(AXES),
            P(AXES),
            P(AXES, None, None),
            P(AXES, None),
            P(AXES, None, None),
        ),
        out_specs=P(None, None, AXES),
        check_vma=False,
    )
```

```python
import functools

import jax
import jax.numpy as jnp
import numpy as np
from jax import lax
from jax.experimental import pallas as pl
from jax.experimental.pallas import tpu as pltpu
from jax.sharding import PartitionSpec as P

AXES = ("slab", "cross")
F32, BF16, I32 = jnp.float32, jnp.bfloat16, jnp.int32
VMEM_BYTES = 36 * 1024 * 1024
ROWS_Q = 168
ROWS_K = 48
HALF = 32
PITCH = 9
ODD_FROM = 1168


def shifted(value, axis):
    count = lax.axis_size(axis)
    return lax.ppermute(value, axis, [(source, source - 1) for source in range(1, count)])


def shifted_both(value):
    slabs, crosses = lax.axis_size("slab"), lax.axis_size("cross")
    pairs = [
        (u * crosses + v, (u - 1) * crosses + v - 1)
        for u in range(1, slabs)
        for v in range(1, crosses)
    ]
    return lax.ppermute(value, AXES, pairs)


def gauss_basis():
    spread = np.sqrt(0.15)
    places = np.array([0.5 - spread, 0.5, 0.5 + spread], np.float32)
    one = np.stack([np.float32(1.0) - places, places], 1).astype(np.float64)
    return np.einsum("ai,bj,ck->abcijk", one, one, one).reshape(27, 8)


def tables():
    q_rows = np.zeros((ROWS_Q, 162), np.float32)
    for m in range(6):
        for g in range(24):
            q_rows[m * 24 + g, 6 * g + m] = 1
        for g in range(3):
            q_rows[144 + (m // 2) * 8 + (m % 2) * 3 + g, 6 * (24 + g) + m] = 1
    cols = np.zeros((108, 3 * ROWS_K), np.float32)
    places = [(0, 0), (0, 1), (1, 0), (1, 1), (2, 0), (2, 1), (0, 2), (1, 2), (2, 2)]
    for i in range(3):
        for place, (j, k) in enumerate(places):
            for c in range(4):
                cols[4 * (9 * i + 3 * j + k) + c, ROWS_K * i + 4 * place + c] = 1
    perm = np.zeros((256, 256), np.float32)
    for f in range(2):
        for d in range(16):
            for s in range(2):
                for c in range(4):
                    perm[(f * 16 + d) * 8 + s * 4 + c, s * 128 + f * 64 + c * 16 + d] = 1
    basis = gauss_basis()
    rows = np.concatenate([basis[:27], basis[24:27], np.zeros((2, 8))], 0).T
    high = rows.astype(np.float32).astype(jnp.bfloat16)
    low = (rows - high.astype(np.float64)).astype(np.float32).astype(jnp.bfloat16)
    eye = np.eye(16)
    block = lambda x: np.einsum("ab,tg->agbt", eye, x.astype(np.float64)).reshape(512, 128)
    split = np.concatenate([block(high), block(low)], 1)
    bf = lambda x: x.astype(jnp.bfloat16)
    return bf(q_rows), bf(cols), bf(perm), bf(split)


def dot(a, b, dims=((1,), (0,))):
    return lax.dot_general(a, b, (dims, ((), ())), preferred_element_type=F32)


def prepare_kernel(order_s, weight, order_v, send, count, placed, slots, turned, spread):
    blocks = weight.shape[1] // 128

    def turn(blk, _):
        at = pl.ds(pl.multiple_of(blk * 128, 128), 128)
        w = weight[:, at]
        rows = jnp.concatenate([w, w[24:27], jnp.zeros((2, 128), F32)], 0)
        turned[at, :] = rows.T
        return 0

    lax.fori_loop(0, blocks, turn, 0, unroll=4)

    def place(step, _):
        found = [turned[pl.ds(step * 16 + r, 1), :] for r in range(16)]
        for r, row in enumerate(found):
            spread[pl.ds(order_s[step * 16 + r], 1), :] = row
        return 0

    lax.fori_loop(0, blocks * 8, place, 0)

    def back(blk, _):
        at = pl.ds(pl.multiple_of(blk * 128, 128), 128)
        placed[blk] = spread[at, :].T
        return 0

    lax.fori_loop(0, blocks, back, 0, unroll=4)
    live = lax.broadcasted_iota(I32, send.shape, 0) < count[...]
    for part in range(send.shape[0] // 8):
        at = slice(part * 8, part * 8 + 8)
        asked = send[at, :]
        low, high = asked & 127, asked >> 7
        found = jnp.zeros(asked.shape, I32)
        for row in range(blocks):
            table = jnp.broadcast_to(order_v[row : row + 1, :], asked.shape)
            found = jnp.where(high == row, jnp.take_along_axis(table, low, axis=1), found)
        slots[at, :] = jnp.where(live[at, :], found, weight.shape[1])


def partial_kernel(
    slots, odd, even, side_odd, side_even, face, corner, weight, smap, qrow, kcol, perm, basis,
    words, flat, flat_side, taps, mapped, top_part, low_part, rows, low_code, high_code,
):
    step = pl.program_id(0)
    last = pl.num_programs(0) - 1
    elem_rows = 4

    @pl.when(step == 0)
    def _():
        wide = dot(qrow[...], smap[...]).astype(BF16)
        mapped[...] = dot(wide, kcol[...]).astype(BF16)

    def fill(where, plane, side):
        for z in range(257):
            at = z % 2 * ODD_FROM + z // 2 * PITCH
            flat[where, at : at + 8, :] = plane[z].astype(F32)
        flat_side[where, 0:257, :] = side.astype(F32)

    def turn(where, slot):
        def line(y, k):
            if y < 8:
                at = k % 2 * ODD_FROM + k // 2 * PITCH + y
                return flat[where, pl.ds(at, 128, stride=PITCH), :].astype(BF16)
            return flat_side[where, pl.ds(k, 128, stride=2), :].astype(BF16)

        def ordered(one, other):
            pair = jnp.concatenate([jnp.concatenate(one, 1), jnp.concatenate(other, 1)], 0)
            both = dot(perm[...], pair, ((1,), (1,)))
            return both[:, :128].reshape(32, 8, 128), both[:, 128:].reshape(32, 8, 128)

        def near(y):
            return line(y, 0), line(y, 1)

        def far(y):
            return line(y, 2), line(min(y + 1, 8), 2)

        before, beyond = ordered(near(0), far(0))
        for b in range(elem_rows):
            y = 2 * b
            held = beyond
            middle, after = ordered(near(y + 1), near(y + 2))
            if b % 2 == 0:
                beyond, later = ordered(far(y + 2), far(y + 4))
            else:
                beyond = later
            at = b * ROWS_K
            taps[slot, :, at : at + 16, :] = jnp.concatenate([before, middle], 1).astype(BF16)
            taps[slot, :, at + 16 : at + 32, :] = jnp.concatenate([after, held], 1).astype(BF16)
            taps[slot, :, at + 32 : at + 48, :] = jnp.concatenate([beyond, beyond], 1).astype(BF16)
            before = after

    @pl.when(step > 0)
    def _():
        fill(0, odd.at[0], side_odd[0])
        turn(0, lax.rem(2 * step + 2, 3))

    @pl.when(step < last)
    def _():
        fill(1, even.at[0], side_even[0])

    @pl.when(step == last)
    def _():
        fill(1, face, corner[...])

    turn(1, lax.rem(2 * step, 3))

    @pl.when(step > 0)
    def _():
        a = step - 1
        plane_slots = [lax.rem(2 * a + i, 3) for i in range(3)]

        def element_row(b, _):
            at = pl.ds(pl.multiple_of(b * ROWS_K, 16), ROWS_K)
            scale = weight[a * elem_rows + b]
            pieces = []
            for d in range(16):
                parts = [
                    jnp.concatenate([taps[s, d, at, :], taps[s, 16 + d, at, :]], 1)
                    for s in plane_slots
                ]
                strain = dot(mapped[...], jnp.concatenate(parts, 0))
                product = strain[:, :128] * strain[:, 128:]
                main = product[0:24]
                for m in range(1, 6):
                    main = main + product[24 * m : 24 * m + 24]
                rest = product[144:152] + product[152:160] + product[160:168]
                summed = jnp.concatenate([main, rest], 0) * scale
                pieces.append(summed)
                if d % 4 == 3:
                    by_elem = jnp.concatenate(pieces, 0).T
                    pieces = []
                    high = by_elem.astype(BF16)
                    to = pl.ds(pl.multiple_of(b * 128, 128), 128)
                    top_part[to, (d - 3) * 32 : (d + 1) * 32] = high
                    low_part[to, (d - 3) * 32 : (d + 1) * 32] = (by_elem - high.astype(F32)).astype(BF16)
            return 0

        lax.fori_loop(0, elem_rows, element_row, 0, unroll=4)
        out_at = pl.ds(pl.multiple_of(a * elem_rows * 128, 128), elem_rows * 128)
        both = dot(top_part[...], basis[...])
        rows[out_at, :] = both[:, :128] + (both[:, 128:] + dot(low_part[...], basis[:, :128]))

    @pl.when(step == last)
    def _():
        count = rows.shape[0]
        chunk = 128

        def largest(i, top):
            block = rows[pl.ds(pl.multiple_of(i * chunk, chunk), chunk), :]
            return jnp.maximum(top, jnp.max(jnp.abs(block).reshape(chunk // 8, 8, 128), 0))

        top = lax.fori_loop(0, count // chunk, largest, jnp.full((8, 128), 1e-30, F32))
        top = jnp.max(jnp.max(top, axis=1, keepdims=True), axis=0, keepdims=True)
        level = jnp.ceil(jnp.log2(jnp.broadcast_to(top, (1, 128))) * 4096.0 + 1.0)
        inverse = jnp.exp2(level * (-1.0 / 4096.0))

        def encode(i, _):
            at = pl.ds(pl.multiple_of(i * chunk, chunk), chunk)
            block = rows[at, :]
            size = jnp.maximum(jnp.abs(block) * inverse, 1e-36)
            root = jnp.exp2(jnp.log2(size) * (1.0 / 3.0)) * 32767.0
            code = jnp.minimum(root + 0.5, 32767.0).astype(I32)
            code = jnp.where(block < 0.0, -code, code)
            low_code[at, :] = code & 65535
            high_code[at, :] = code << 16
            return 0

        lax.fori_loop(0, count // chunk, encode, 0)
        low_code[count : count + 8, :] = jnp.zeros((8, 128), I32)
        high_code[count : count + 8, :] = jnp.zeros((8, 128), I32)

        def gather(o, _):
            first_row = o * (HALF + 1)

            for group in range(0, HALF, 16):
                found = []
                for j in range(group, group + 16):
                    first = low_code[pl.ds(slots[2 * j, o], 1), :]
                    found.append(first | high_code[pl.ds(slots[2 * j + 1, o], 1), :])
                for r, word in enumerate(found):
                    words[pl.ds(first_row + group + r, 1), :] = word
            words[pl.ds(first_row + HALF, 1), :] = level.astype(I32)
            return 0

        lax.fori_loop(0, words.shape[0] // (HALF + 1), gather, 0)


def collect_kernel(cells, words, param, out, made, sent, *sums):
    count = out.shape[1]

    def clear(i, _):
        for total in sums:
            total[pl.ds(pl.multiple_of(i * 128, 128), 128), :] = jnp.zeros((128, 128), F32)
        return 0

    lax.fori_loop(0, count // 128, clear, 0)

    senders = words.shape[0] // (HALF + 1)

    def scale_of(p):
        level = words[pl.ds(p * (HALF + 1) + HALF, 1), :].astype(F32)
        return jnp.exp2(level * (1.0 / 4096.0)) * (1.0 / 32767.0**3)

    def add(p, scale):
        after = scale_of(jnp.minimum(p + 1, senders - 1))
        first_row = p * (HALF + 1)
        for group in range(0, HALF, 8):
            found = [words[pl.ds(first_row + group + r, 1), :] for r in range(8)]
            values = []
            for word in found:
                for half in (word << 16, word):
                    code = lax.shift_right_arithmetic(half, 16).astype(F32)
                    values.append(code * code * (code * scale))
            for r in range(0, 16, 4):
                ats = [pl.ds(cells[2 * group + r + t, p], 1) for t in range(4)]
                held = [total[at, :] for total, at in zip(sums, ats)]
                for total, at, was, value in zip(sums, ats, held, values[r : r + 4]):
                    total[at, :] = was + value
        return after

    lax.fori_loop(0, senders, add, scale_of(0), unroll=2)

    copies = []
    width = count // sent.shape[0]
    for part in range(sent.shape[0]):

        def finish(i, _):
            at = pl.ds(pl.multiple_of(i * 128, 128), 128)
            total = (sums[0][at, :] + sums[1][at, :]) + (sums[2][at, :] + sums[3][at, :])
            made[:, at] = total.T * jnp.exp(param[pl.ds(i, 1), :])
            return 0

        lax.fori_loop(part * width // 128, (part + 1) * width // 128, finish, 0, unroll=4)
        at = pl.ds(part * width, width)
        copies.append(pltpu.make_async_copy(made.at[:, at], out.at[:, at], sent.at[part]))
        copies[-1].start()
    for copy in copies:
        copy.wait()


def whole(shape):
    zeros = (0,) * len(shape)
    return pl.BlockSpec(shape, lambda *_: zeros)


def on_device(fields, strain_map, quad_weight, param, elem_order, send_elem, send_count, recv_cell):
    planes = jnp.transpose(fields, (0, 2, 1, 3))
    face = jnp.transpose(shifted(fields[0:1], "slab"), (0, 2, 1, 3))[0]
    corner = shifted_both(fields[0:1, 0:1])[0, 0]
    side = shifted(fields[:, 0:1], "cross")[:, 0]
    q_rows, k_cols, perm, basis = tables()
    elems = elem_order.shape[0]
    smem = pl.BlockSpec(memory_space=pltpu.SMEM)
    vmem = pl.BlockSpec(memory_space=pltpu.VMEM)
    params = pltpu.CompilerParams(vmem_limit_bytes=VMEM_BYTES)

    placed, slots = pl.pallas_call(
        prepare_kernel,
        out_shape=(
            jax.ShapeDtypeStruct((elems // 128, 32, 128), F32),
            jax.ShapeDtypeStruct((64, 128), I32),
        ),
        in_specs=[smem] + [vmem] * 4,
        out_specs=(vmem, vmem),
        scratch_shapes=[pltpu.VMEM((elems, 32), F32), pltpu.VMEM((elems, 32), F32)],
        compiler_params=params,
    )(elem_order, quad_weight, elem_order.reshape(elems // 128, 128), send_elem[0].T, send_count)

    block = (1, 257, 8, 128)
    side_block = (1, 257, 128)
    odd = lambda s: jnp.maximum(2 * s - 1, 1)
    even = lambda s: jnp.minimum(2 * s, 14)
    words = pl.pallas_call(
        partial_kernel,
        grid=(9,),
        out_shape=jax.ShapeDtypeStruct((128 * 33, 128), I32),
        in_specs=[
            smem,
            pl.BlockSpec(block, lambda s: (odd(s), 0, 0, 0)),
            pl.BlockSpec(block, lambda s: (even(s), 0, 0, 0)),
            pl.BlockSpec(side_block, lambda s: (odd(s), 0, 0)),
            pl.BlockSpec(side_block, lambda s: (even(s), 0, 0)),
            whole((257, 8, 128)),
            whole((257, 128)),
            whole(placed.shape),
            whole(strain_map.shape),
            whole(q_rows.shape),
            whole(k_cols.shape),
            whole(perm.shape),
            whole(basis.shape),
        ],
        out_specs=whole((128 * 33, 128)),
        scratch_shapes=[
            pltpu.VMEM((2, 2 * ODD_FROM, 128), F32),
            pltpu.VMEM((2, 264, 128), F32),
            pltpu.VMEM((3, 32, 4 * ROWS_K, 128), BF16),
            pltpu.VMEM((ROWS_Q, 3 * ROWS_K), BF16),
            pltpu.VMEM((512, 512), BF16),
            pltpu.VMEM((512, 512), BF16),
            pltpu.VMEM((elems, 128), F32),
            pltpu.VMEM((elems + 8, 128), I32),
            pltpu.VMEM((elems + 8, 128), I32),
        ],
        compiler_params=params,
    )(slots, planes, planes, side, side, face, corner, placed, strain_map, q_rows, k_cols, perm, basis)

    arrived = lax.all_to_all(words.reshape(128, 33, 1, 128), AXES, split_axis=0, concat_axis=0, tiled=True)
    cells = param.shape[0]
    terms = pl.pallas_call(
        collect_kernel,
        out_shape=jax.ShapeDtypeStruct((128, cells), F32),
        in_specs=[smem, vmem, vmem],
        out_specs=pl.BlockSpec(memory_space=pl.ANY),
        scratch_shapes=[pltpu.VMEM((128, cells), F32), pltpu.SemaphoreType.DMA((8,))]
        + [pltpu.VMEM((cells, 128), F32)] * 4,
        compiler_params=params,
    )(recv_cell[0].T, arrived.reshape(128 * 33, 128), param.reshape(cells // 128, 128))
    return terms.reshape(16, 8, cells)


def solution(mesh):
    return jax.shard_map(
        on_device,
        mesh=mesh,
        in_specs=(
            P("slab", "cross", None, None),
            P(),
            P(None, AXES),
            P(AXES),
            P(AXES),
            P(AXES, None, None),
            P(AXES, None),
            P(AXES, None, None),
        ),
        out_specs=P(None, None, AXES),
        check_vma=False,
    )
```

```python
import functools

import jax
import jax.numpy as jnp
import numpy as np
from jax import lax
from jax.experimental import pallas as pl
from jax.experimental.pallas import tpu as pltpu
from jax.sharding import PartitionSpec as P

AXES = ("slab", "cross")
F32, BF16, I32 = jnp.float32, jnp.bfloat16, jnp.int32
VMEM_BYTES = 36 * 1024 * 1024
ROWS_Q = 168
ROWS_K = 48
HALF = 32
PITCH = 9
ODD_FROM = 1168


def shifted(value, axis):
    count = lax.axis_size(axis)
    return lax.ppermute(value, axis, [(source, source - 1) for source in range(1, count)])


def shifted_both(value):
    slabs, crosses = lax.axis_size("slab"), lax.axis_size("cross")
    pairs = [
        (u * crosses + v, (u - 1) * crosses + v - 1)
        for u in range(1, slabs)
        for v in range(1, crosses)
    ]
    return lax.ppermute(value, AXES, pairs)


def gauss_basis():
    spread = np.sqrt(0.15)
    places = np.array([0.5 - spread, 0.5, 0.5 + spread], np.float32)
    one = np.stack([np.float32(1.0) - places, places], 1).astype(np.float64)
    return np.einsum("ai,bj,ck->abcijk", one, one, one).reshape(27, 8)


def tables():
    q_rows = np.zeros((ROWS_Q, 162), np.float32)
    for m in range(6):
        for g in range(24):
            q_rows[m * 24 + g, 6 * g + m] = 1
        for g in range(3):
            q_rows[144 + (m // 2) * 8 + (m % 2) * 3 + g, 6 * (24 + g) + m] = 1
    cols = np.zeros((108, 3 * ROWS_K), np.float32)
    places = [(0, 0), (0, 1), (1, 0), (1, 1), (2, 0), (2, 1), (0, 2), (1, 2), (2, 2)]
    for i in range(3):
        for place, (j, k) in enumerate(places):
            for c in range(4):
                cols[4 * (9 * i + 3 * j + k) + c, ROWS_K * i + 4 * place + c] = 1
    perm = np.zeros((256, 256), np.float32)
    for f in range(2):
        for d in range(16):
            for s in range(2):
                for c in range(4):
                    perm[(f * 16 + d) * 8 + s * 4 + c, s * 128 + f * 64 + c * 16 + d] = 1
    basis = gauss_basis()
    rows = np.concatenate([basis[:27], basis[24:27], np.zeros((2, 8))], 0).T
    high = rows.astype(np.float32).astype(jnp.bfloat16)
    low = (rows - high.astype(np.float64)).astype(np.float32).astype(jnp.bfloat16)
    eye = np.eye(16)
    block = lambda x: np.einsum("ab,tg->agbt", eye, x.astype(np.float64)).reshape(512, 128)
    split = np.concatenate([block(high), block(low)], 1)
    bf = lambda x: x.astype(jnp.bfloat16)
    return bf(q_rows), bf(cols), bf(perm), bf(split)


def dot(a, b, dims=((1,), (0,))):
    return lax.dot_general(a, b, (dims, ((), ())), preferred_element_type=F32)


def paired(upper, lower):
    return upper | (lower << 16)


def prepare_kernel(
    order_s, weight, order_v, send, count, cells, placed, slots, places, turned, spread
):
    blocks = weight.shape[1] // 128

    def turn(blk, _):
        at = pl.ds(pl.multiple_of(blk * 128, 128), 128)
        w = weight[:, at]
        rows = jnp.concatenate([w, w[24:27], jnp.zeros((2, 128), F32)], 0)
        turned[at, :] = rows.T
        return 0

    lax.fori_loop(0, blocks, turn, 0, unroll=4)

    def place(step, _):
        found = [turned[pl.ds(step * 16 + r, 1), :] for r in range(16)]
        for r, row in enumerate(found):
            spread[pl.ds(order_s[step * 16 + r], 1), :] = row
        return 0

    lax.fori_loop(0, blocks * 8, place, 0)

    def back(blk, _):
        at = pl.ds(pl.multiple_of(blk * 128, 128), 128)
        placed[blk] = spread[at, :].T
        return 0

    lax.fori_loop(0, blocks, back, 0, unroll=4)
    live = lax.broadcasted_iota(I32, send.shape, 0) < count[...]
    looked_up = []
    for part in range(send.shape[0] // 8):
        at = slice(part * 8, part * 8 + 8)
        asked = send[at, :]
        low, high = asked & 127, asked >> 7
        found = jnp.zeros(asked.shape, I32)
        for row in range(blocks):
            table = jnp.broadcast_to(order_v[row : row + 1, :], asked.shape)
            found = jnp.where(high == row, jnp.take_along_axis(table, low, axis=1), found)
        looked_up.append(jnp.where(live[at, :], found, weight.shape[1]))
    for part in range(HALF // 8):
        at = slice(part * 8, part * 8 + 8)
        slots[at, :] = paired(looked_up[part], looked_up[part + HALF // 8])
    places[...] = paired(cells[:HALF, :], cells[HALF:, :])


def partial_kernel(
    slots, odd, even, side_odd, side_even, face, corner, weight, smap, qrow, kcol, perm, basis,
    words, flat, flat_side, taps, mapped, top_part, low_part, rows, low_code, high_code,
):
    step = pl.program_id(0)
    last = pl.num_programs(0) - 1
    elem_rows = 4

    @pl.when(step == 0)
    def _():
        wide = dot(qrow[...], smap[...]).astype(BF16)
        mapped[...] = dot(wide, kcol[...]).astype(BF16)

    def fill(where, plane, side):
        for z in range(257):
            at = z % 2 * ODD_FROM + z // 2 * PITCH
            flat[where, at : at + 8, :] = plane[z].astype(F32)
        flat_side[where, 0:257, :] = side.astype(F32)

    def turn(where, slot):
        def line(y, k):
            if y < 8:
                at = k % 2 * ODD_FROM + k // 2 * PITCH + y
                return flat[where, pl.ds(at, 128, stride=PITCH), :].astype(BF16)
            return flat_side[where, pl.ds(k, 128, stride=2), :].astype(BF16)

        def ordered(one, other):
            pair = jnp.concatenate([jnp.concatenate(one, 1), jnp.concatenate(other, 1)], 0)
            both = dot(perm[...], pair, ((1,), (1,)))
            return both[:, :128].reshape(32, 8, 128), both[:, 128:].reshape(32, 8, 128)

        def near(y):
            return line(y, 0), line(y, 1)

        def far(y):
            return line(y, 2), line(min(y + 1, 8), 2)

        before, beyond = ordered(near(0), far(0))
        for b in range(elem_rows):
            y = 2 * b
            held = beyond
            middle, after = ordered(near(y + 1), near(y + 2))
            if b % 2 == 0:
                beyond, later = ordered(far(y + 2), far(y + 4))
            else:
                beyond = later
            at = b * ROWS_K
            taps[slot, :, at : at + 16, :] = jnp.concatenate([before, middle], 1).astype(BF16)
            taps[slot, :, at + 16 : at + 32, :] = jnp.concatenate([after, held], 1).astype(BF16)
            taps[slot, :, at + 32 : at + 48, :] = jnp.concatenate([beyond, beyond], 1).astype(BF16)
            before = after

    @pl.when(step > 0)
    def _():
        fill(0, odd.at[0], side_odd[0])
        turn(0, lax.rem(2 * step + 2, 3))

    @pl.when(step < last)
    def _():
        fill(1, even.at[0], side_even[0])

    @pl.when(step == last)
    def _():
        fill(1, face, corner[...])

    turn(1, lax.rem(2 * step, 3))

    @pl.when(step > 0)
    def _():
        a = step - 1
        plane_slots = [lax.rem(2 * a + i, 3) for i in range(3)]

        def element_row(b, _):
            at = pl.ds(pl.multiple_of(b * ROWS_K, 16), ROWS_K)
            scale = weight[a * elem_rows + b]
            pieces = []
            for d in range(16):
                parts = [
                    jnp.concatenate([taps[s, d, at, :], taps[s, 16 + d, at, :]], 1)
                    for s in plane_slots
                ]
                strain = dot(mapped[...], jnp.concatenate(parts, 0))
                product = strain[:, :128] * strain[:, 128:]
                main = product[0:24]
                for m in range(1, 6):
                    main = main + product[24 * m : 24 * m + 24]
                rest = product[144:152] + product[152:160] + product[160:168]
                summed = jnp.concatenate([main, rest], 0) * scale
                pieces.append(summed)
                if d % 4 == 3:
                    by_elem = jnp.concatenate(pieces, 0).T
                    pieces = []
                    high = by_elem.astype(BF16)
                    to = pl.ds(pl.multiple_of(b * 128, 128), 128)
                    top_part[to, (d - 3) * 32 : (d + 1) * 32] = high
                    low_part[to, (d - 3) * 32 : (d + 1) * 32] = (by_elem - high.astype(F32)).astype(BF16)
            return 0

        lax.fori_loop(0, elem_rows, element_row, 0, unroll=4)
        out_at = pl.ds(pl.multiple_of(a * elem_rows * 128, 128), elem_rows * 128)
        both = dot(top_part[...], basis[...])
        rows[out_at, :] = both[:, :128] + (both[:, 128:] + dot(low_part[...], basis[:, :128]))

    @pl.when(step == last)
    def _():
        count = rows.shape[0]
        chunk = 128

        def largest(i, top):
            block = rows[pl.ds(pl.multiple_of(i * chunk, chunk), chunk), :]
            return jnp.maximum(top, jnp.max(jnp.abs(block).reshape(chunk // 8, 8, 128), 0))

        top = lax.fori_loop(0, count // chunk, largest, jnp.full((8, 128), 1e-30, F32))
        top = jnp.max(jnp.max(top, axis=1, keepdims=True), axis=0, keepdims=True)
        level = jnp.ceil(jnp.log2(jnp.broadcast_to(top, (1, 128))) * 4096.0 + 1.0)
        inverse = jnp.exp2(level * (-1.0 / 4096.0))

        def encode(i, _):
            at = pl.ds(pl.multiple_of(i * chunk, chunk), chunk)
            block = rows[at, :]
            size = jnp.maximum(jnp.abs(block) * inverse, 1e-36)
            root = jnp.exp2(jnp.log2(size) * (1.0 / 3.0)) * 32767.0
            code = jnp.minimum(root + 0.5, 32767.0).astype(I32)
            code = jnp.where(block < 0.0, -code, code)
            low_code[at, :] = code & 65535
            high_code[at, :] = code << 16
            return 0

        lax.fori_loop(0, count // chunk, encode, 0)
        low_code[count : count + 8, :] = jnp.zeros((8, 128), I32)
        high_code[count : count + 8, :] = jnp.zeros((8, 128), I32)

        def gather(o, _):
            first_row = o * (HALF + 1)

            for group in range(0, HALF, 16):
                found = []
                for j in range(group, group + 16):
                    pair = slots[j, o]
                    first = low_code[pl.ds(pair & 65535, 1), :]
                    found.append(first | high_code[pl.ds(lax.shift_right_logical(pair, 16), 1), :])
                for r, word in enumerate(found):
                    words[pl.ds(first_row + group + r, 1), :] = word
            words[pl.ds(first_row + HALF, 1), :] = level.astype(I32)
            return 0

        lax.fori_loop(0, words.shape[0] // (HALF + 1), gather, 0)


def collect_kernel(cells, words, param, out, made, sent, *sums):
    count = out.shape[1]

    def clear(i, _):
        for total in sums:
            total[pl.ds(pl.multiple_of(i * 128, 128), 128), :] = jnp.zeros((128, 128), F32)
        return 0

    lax.fori_loop(0, count // 128, clear, 0)

    senders = words.shape[0] // (HALF + 1)

    def scale_of(p):
        level = words[pl.ds(p * (HALF + 1) + HALF, 1), :].astype(F32)
        return jnp.exp2(level * (1.0 / 4096.0)) * (1.0 / 32767.0**3)

    def add(p, scale):
        after = scale_of(jnp.minimum(p + 1, senders - 1))
        first_row = p * (HALF + 1)
        for group in range(0, HALF, 8):
            found = [words[pl.ds(first_row + group + r, 1), :] for r in range(8)]
            values = []
            for word in found:
                for half in (word << 16, word):
                    code = lax.shift_right_arithmetic(half, 16).astype(F32)
                    values.append(code * code * (code * scale))
            for r in range(0, 16, 4):
                pairs = [cells[group + r // 2 + t, p] for t in range(2)]
                ats = [
                    pl.ds(at, 1)
                    for pair in pairs
                    for at in (pair & 65535, lax.shift_right_logical(pair, 16))
                ]
                held = [total[at, :] for total, at in zip(sums, ats)]
                for total, at, was, value in zip(sums, ats, held, values[r : r + 4]):
                    total[at, :] = was + value
        return after

    lax.fori_loop(0, senders, add, scale_of(0), unroll=2)

    copies = []
    width = count // sent.shape[0]
    for part in range(sent.shape[0]):

        def finish(i, _):
            at = pl.ds(pl.multiple_of(i * 128, 128), 128)
            total = (sums[0][at, :] + sums[1][at, :]) + (sums[2][at, :] + sums[3][at, :])
            made[:, at] = total.T * jnp.exp(param[pl.ds(i, 1), :])
            return 0

        lax.fori_loop(part * width // 128, (part + 1) * width // 128, finish, 0, unroll=4)
        at = pl.ds(part * width, width)
        copies.append(pltpu.make_async_copy(made.at[:, at], out.at[:, at], sent.at[part]))
        copies[-1].start()
    for copy in copies:
        copy.wait()


def whole(shape):
    zeros = (0,) * len(shape)
    return pl.BlockSpec(shape, lambda *_: zeros)


def on_device(fields, strain_map, quad_weight, param, elem_order, send_elem, send_count, recv_cell):
    planes = jnp.transpose(fields, (0, 2, 1, 3))
    face = jnp.transpose(shifted(fields[0:1], "slab"), (0, 2, 1, 3))[0]
    corner = shifted_both(fields[0:1, 0:1])[0, 0]
    side = shifted(fields[:, 0:1], "cross")[:, 0]
    q_rows, k_cols, perm, basis = tables()
    elems = elem_order.shape[0]
    smem = pl.BlockSpec(memory_space=pltpu.SMEM)
    vmem = pl.BlockSpec(memory_space=pltpu.VMEM)
    params = pltpu.CompilerParams(vmem_limit_bytes=VMEM_BYTES)

    placed, slots, places = pl.pallas_call(
        prepare_kernel,
        out_shape=(
            jax.ShapeDtypeStruct((elems // 128, 32, 128), F32),
            jax.ShapeDtypeStruct((HALF, 128), I32),
            jax.ShapeDtypeStruct((HALF, 128), I32),
        ),
        in_specs=[smem] + [vmem] * 5,
        out_specs=(vmem, vmem, vmem),
        scratch_shapes=[pltpu.VMEM((elems, 32), F32), pltpu.VMEM((elems, 32), F32)],
        compiler_params=params,
    )(elem_order, quad_weight, elem_order.reshape(elems // 128, 128), send_elem[0].T, send_count, recv_cell[0].T)

    block = (1, 257, 8, 128)
    side_block = (1, 257, 128)
    odd = lambda s: jnp.maximum(2 * s - 1, 1)
    even = lambda s: jnp.minimum(2 * s, 14)
    words = pl.pallas_call(
        partial_kernel,
        grid=(9,),
        out_shape=jax.ShapeDtypeStruct((128 * 33, 128), I32),
        in_specs=[
            smem,
            pl.BlockSpec(block, lambda s: (odd(s), 0, 0, 0)),
            pl.BlockSpec(block, lambda s: (even(s), 0, 0, 0)),
            pl.BlockSpec(side_block, lambda s: (odd(s), 0, 0)),
            pl.BlockSpec(side_block, lambda s: (even(s), 0, 0)),
            whole((257, 8, 128)),
            whole((257, 128)),
            whole(placed.shape),
            whole(strain_map.shape),
            whole(q_rows.shape),
            whole(k_cols.shape),
            whole(perm.shape),
            whole(basis.shape),
        ],
        out_specs=whole((128 * 33, 128)),
        scratch_shapes=[
            pltpu.VMEM((2, 2 * ODD_FROM, 128), F32),
            pltpu.VMEM((2, 264, 128), F32),
            pltpu.VMEM((3, 32, 4 * ROWS_K, 128), BF16),
            pltpu.VMEM((ROWS_Q, 3 * ROWS_K), BF16),
            pltpu.VMEM((512, 512), BF16),
            pltpu.VMEM((512, 512), BF16),
            pltpu.VMEM((elems, 128), F32),
            pltpu.VMEM((elems + 8, 128), I32),
            pltpu.VMEM((elems + 8, 128), I32),
        ],
        compiler_params=params,
    )(slots, planes, planes, side, side, face, corner, placed, strain_map, q_rows, k_cols, perm, basis)

    arrived = lax.all_to_all(words.reshape(128, 33, 1, 128), AXES, split_axis=0, concat_axis=0, tiled=True)
    cells = param.shape[0]
    terms = pl.pallas_call(
        collect_kernel,
        out_shape=jax.ShapeDtypeStruct((128, cells), F32),
        in_specs=[smem, vmem, vmem],
        out_specs=pl.BlockSpec(memory_space=pl.ANY),
        scratch_shapes=[pltpu.VMEM((128, cells), F32), pltpu.SemaphoreType.DMA((8,))]
        + [pltpu.VMEM((cells, 128), F32)] * 4,
        compiler_params=params,
    )(places, arrived.reshape(128 * 33, 128), param.reshape(cells // 128, 128))
    return terms.reshape(16, 8, cells)


def solution(mesh):
    return jax.shard_map(
        on_device,
        mesh=mesh,
        in_specs=(
            P("slab", "cross", None, None),
            P(),
            P(None, AXES),
            P(AXES),
            P(AXES),
            P(AXES, None, None),
            P(AXES, None),
            P(AXES, None, None),
        ),
        out_specs=P(None, None, AXES),
        check_vma=False,
    )
```

```python
import functools

import jax
import jax.numpy as jnp
import numpy as np
from jax import lax
from jax.experimental import pallas as pl
from jax.experimental.pallas import tpu as pltpu
from jax.sharding import PartitionSpec as P

AXES = ("slab", "cross")
F32, BF16, I32 = jnp.float32, jnp.bfloat16, jnp.int32
VMEM_BYTES = 36 * 1024 * 1024
ROWS_Q = 168
ROWS_K = 48
HALF = 32
PITCH = 9
ODD_FROM = 1168


def shifted(value, axis):
    count = lax.axis_size(axis)
    return lax.ppermute(value, axis, [(source, source - 1) for source in range(1, count)])


def shifted_both(value):
    slabs, crosses = lax.axis_size("slab"), lax.axis_size("cross")
    pairs = [
        (u * crosses + v, (u - 1) * crosses + v - 1)
        for u in range(1, slabs)
        for v in range(1, crosses)
    ]
    return lax.ppermute(value, AXES, pairs)


def gauss_basis():
    spread = np.sqrt(0.15)
    places = np.array([0.5 - spread, 0.5, 0.5 + spread], np.float32)
    one = np.stack([np.float32(1.0) - places, places], 1).astype(np.float64)
    return np.einsum("ai,bj,ck->abcijk", one, one, one).reshape(27, 8)


def tables():
    q_rows = np.zeros((ROWS_Q, 162), np.float32)
    for m in range(6):
        for g in range(24):
            q_rows[m * 24 + g, 6 * g + m] = 1
        for g in range(3):
            q_rows[144 + (m // 2) * 8 + (m % 2) * 3 + g, 6 * (24 + g) + m] = 1
    cols = np.zeros((108, 3 * ROWS_K), np.float32)
    places = [(0, 0), (0, 1), (1, 0), (1, 1), (2, 0), (2, 1), (0, 2), (1, 2), (2, 2)]
    for i in range(3):
        for place, (j, k) in enumerate(places):
            for c in range(4):
                row = 4 * place + (8 if place == 8 else 0)
                cols[4 * (9 * i + 3 * j + k) + c, ROWS_K * i + row + c] = 1
    perm = np.zeros((256, 256), np.float32)
    for f in range(2):
        for d in range(16):
            for s in range(2):
                for c in range(4):
                    perm[(f * 16 + d) * 8 + s * 4 + c, s * 128 + f * 64 + c * 16 + d] = 1
    basis = gauss_basis()
    rows = np.concatenate([basis[:27], basis[24:27], np.zeros((2, 8))], 0).T
    high = rows.astype(np.float32).astype(jnp.bfloat16)
    low = (rows - high.astype(np.float64)).astype(np.float32).astype(jnp.bfloat16)
    eye = np.eye(16)
    block = lambda x: np.einsum("ab,tg->agbt", eye, x.astype(np.float64)).reshape(512, 128)
    split = np.concatenate([block(high), block(low)], 1)
    bf = lambda x: x.astype(jnp.bfloat16)
    return bf(q_rows), bf(cols), bf(perm), bf(split)


def dot(a, b, dims=((1,), (0,))):
    return lax.dot_general(a, b, (dims, ((), ())), preferred_element_type=F32)


def paired(upper, lower):
    return upper | (lower << 16)


def prepare_kernel(
    order_s, weight, order_v, send, count, cells, placed, slots, places, turned, spread
):
    blocks = weight.shape[1] // 128

    def turn(blk, _):
        at = pl.ds(pl.multiple_of(blk * 128, 128), 128)
        w = weight[:, at]
        rows = jnp.concatenate([w, w[24:27], jnp.zeros((2, 128), F32)], 0)
        turned[at, :] = rows.T
        return 0

    lax.fori_loop(0, blocks, turn, 0, unroll=4)

    def place(step, _):
        found = [turned[pl.ds(step * 16 + r, 1), :] for r in range(16)]
        for r, row in enumerate(found):
            spread[pl.ds(order_s[step * 16 + r], 1), :] = row
        return 0

    lax.fori_loop(0, blocks * 8, place, 0)

    def back(blk, _):
        at = pl.ds(pl.multiple_of(blk * 128, 128), 128)
        placed[blk] = spread[at, :].T
        return 0

    lax.fori_loop(0, blocks, back, 0, unroll=4)
    live = lax.broadcasted_iota(I32, send.shape, 0) < count[...]
    looked_up = []
    for part in range(send.shape[0] // 8):
        at = slice(part * 8, part * 8 + 8)
        asked = send[at, :]
        low, high = asked & 127, asked >> 7
        found = jnp.zeros(asked.shape, I32)
        for row in range(blocks):
            table = jnp.broadcast_to(order_v[row : row + 1, :], asked.shape)
            found = jnp.where(high == row, jnp.take_along_axis(table, low, axis=1), found)
        looked_up.append(jnp.where(live[at, :], found, weight.shape[1]))
    for part in range(HALF // 8):
        at = slice(part * 8, part * 8 + 8)
        slots[at, :] = paired(looked_up[part], looked_up[part + HALF // 8])
    places[...] = paired(cells[:HALF, :], cells[HALF:, :])


def partial_kernel(
    slots, odd, even, side_odd, side_even, face, corner, weight, smap, qrow, kcol, perm, basis,
    words, flat, flat_side, taps, mapped, top_part, low_part, rows, low_code, high_code,
):
    step = pl.program_id(0)
    last = pl.num_programs(0) - 1
    elem_rows = 4

    @pl.when(step == 0)
    def _():
        wide = dot(qrow[...], smap[...]).astype(BF16)
        mapped[...] = dot(wide, kcol[...]).astype(BF16)

    def fill(where, plane, side):
        for z in range(257):
            at = z % 2 * ODD_FROM + z // 2 * PITCH
            flat[where, at : at + 8, :] = plane[z].astype(F32)
        flat_side[where, 0:257, :] = side.astype(F32)

    def turn(where, slot):
        def line(y, k):
            if y < 8:
                at = k % 2 * ODD_FROM + k // 2 * PITCH + y
                return flat[where, pl.ds(at, 128, stride=PITCH), :].astype(BF16)
            return flat_side[where, pl.ds(k, 128, stride=2), :].astype(BF16)

        def ordered(one, other):
            pair = jnp.concatenate([jnp.concatenate(one, 1), jnp.concatenate(other, 1)], 0)
            both = dot(perm[...], pair, ((1,), (1,)))
            return both[:, :128].reshape(32, 8, 128), both[:, 128:].reshape(32, 8, 128)

        def near(y):
            return line(y, 0), line(y, 1)

        def far(y):
            return line(y, 2), line(min(y + 1, 8), 2)

        before, beyond = ordered(near(0), far(0))
        for b in range(elem_rows):
            y = 2 * b
            held = beyond
            middle, after = ordered(near(y + 1), near(y + 2))
            if b % 2 == 0:
                beyond, later = ordered(far(y + 2), far(y + 4))
            else:
                beyond = later
            at = b * 32
            taps[slot, :, at : at + 16, :] = jnp.concatenate([before, middle], 1).astype(BF16)
            taps[slot, :, at + 16 : at + 32, :] = jnp.concatenate([after, held], 1).astype(BF16)
            before = after
        last_tile = jnp.concatenate([beyond, beyond], 1).astype(BF16)
        taps[slot, :, 32 * elem_rows + 16 : 32 * elem_rows + 32, :] = last_tile

    @pl.when(step > 0)
    def _():
        fill(0, odd.at[0], side_odd[0])
        turn(0, lax.rem(2 * step + 2, 3))

    @pl.when(step < last)
    def _():
        fill(1, even.at[0], side_even[0])

    @pl.when(step == last)
    def _():
        fill(1, face, corner[...])

    turn(1, lax.rem(2 * step, 3))

    @pl.when(step > 0)
    def _():
        a = step - 1
        plane_slots = [lax.rem(2 * a + i, 3) for i in range(3)]

        def element_row(b, _):
            near = pl.ds(pl.multiple_of(b * 32, 16), 32)
            next_far = pl.ds(pl.multiple_of(b * 32 + 48, 16), 16)
            scale = weight[a * elem_rows + b]
            pieces = []
            for d in range(16):
                parts = [
                    jnp.concatenate([taps[s, d, at, :], taps[s, 16 + d, at, :]], 1)
                    for s in plane_slots
                    for at in (near, next_far)
                ]
                strain = dot(mapped[...], jnp.concatenate(parts, 0))
                product = strain[:, :128] * strain[:, 128:]
                main = product[0:24]
                for m in range(1, 6):
                    main = main + product[24 * m : 24 * m + 24]
                rest = product[144:152] + product[152:160] + product[160:168]
                summed = jnp.concatenate([main, rest], 0) * scale
                pieces.append(summed)
                if d % 4 == 3:
                    by_elem = jnp.concatenate(pieces, 0).T
                    pieces = []
                    high = by_elem.astype(BF16)
                    to = pl.ds(pl.multiple_of(b * 128, 128), 128)
                    top_part[to, (d - 3) * 32 : (d + 1) * 32] = high
                    low_part[to, (d - 3) * 32 : (d + 1) * 32] = (by_elem - high.astype(F32)).astype(BF16)
            return 0

        lax.fori_loop(0, elem_rows, element_row, 0, unroll=4)
        out_at = pl.ds(pl.multiple_of(a * elem_rows * 128, 128), elem_rows * 128)
        both = dot(top_part[...], basis[...])
        rows[out_at, :] = both[:, :128] + (both[:, 128:] + dot(low_part[...], basis[:, :128]))

    @pl.when(step == last)
    def _():
        count = rows.shape[0]
        chunk = 128

        def largest(i, top):
            block = rows[pl.ds(pl.multiple_of(i * chunk, chunk), chunk), :]
            return jnp.maximum(top, jnp.max(jnp.abs(block).reshape(chunk // 8, 8, 128), 0))

        top = lax.fori_loop(0, count // chunk, largest, jnp.full((8, 128), 1e-30, F32))
        top = jnp.max(jnp.max(top, axis=1, keepdims=True), axis=0, keepdims=True)
        level = jnp.ceil(jnp.log2(jnp.broadcast_to(top, (1, 128))) * 4096.0 + 1.0)
        inverse = jnp.exp2(level * (-1.0 / 4096.0))

        def encode(i, _):
            at = pl.ds(pl.multiple_of(i * chunk, chunk), chunk)
            block = rows[at, :]
            size = jnp.maximum(jnp.abs(block) * inverse, 1e-36)
            root = jnp.exp2(jnp.log2(size) * (1.0 / 3.0)) * 32767.0
            code = jnp.minimum(root + 0.5, 32767.0).astype(I32)
            code = jnp.where(block < 0.0, -code, code)
            low_code[at, :] = code & 65535
            high_code[at, :] = code << 16
            return 0

        lax.fori_loop(0, count // chunk, encode, 0)
        low_code[count : count + 8, :] = jnp.zeros((8, 128), I32)
        high_code[count : count + 8, :] = jnp.zeros((8, 128), I32)

        def gather(o, _):
            first_row = o * (HALF + 1)

            for group in range(0, HALF, 16):
                found = []
                for j in range(group, group + 16):
                    pair = slots[j, o]
                    first = low_code[pl.ds(pair & 65535, 1), :]
                    found.append(first | high_code[pl.ds(lax.shift_right_logical(pair, 16), 1), :])
                for r, word in enumerate(found):
                    words[pl.ds(first_row + group + r, 1), :] = word
            words[pl.ds(first_row + HALF, 1), :] = level.astype(I32)
            return 0

        lax.fori_loop(0, words.shape[0] // (HALF + 1), gather, 0)


def collect_kernel(cells, words, param, out, made, sent, *sums):
    count = out.shape[1]

    def clear(i, _):
        for total in sums:
            total[pl.ds(pl.multiple_of(i * 128, 128), 128), :] = jnp.zeros((128, 128), F32)
        return 0

    lax.fori_loop(0, count // 128, clear, 0)

    senders = words.shape[0] // (HALF + 1)

    def scale_of(p):
        level = words[pl.ds(p * (HALF + 1) + HALF, 1), :].astype(F32)
        return jnp.exp2(level * (1.0 / 4096.0)) * (1.0 / 32767.0**3)

    def add(p, scale):
        after = scale_of(jnp.minimum(p + 1, senders - 1))
        first_row = p * (HALF + 1)
        for group in range(0, HALF, 8):
            found = [words[pl.ds(first_row + group + r, 1), :] for r in range(8)]
            values = []
            for word in found:
                for half in (word << 16, word):
                    code = lax.shift_right_arithmetic(half, 16).astype(F32)
                    values.append(code * code * (code * scale))
            for r in range(0, 16, 4):
                pairs = [cells[group + r // 2 + t, p] for t in range(2)]
                ats = [
                    pl.ds(at, 1)
                    for pair in pairs
                    for at in (pair & 65535, lax.shift_right_logical(pair, 16))
                ]
                held = [total[at, :] for total, at in zip(sums, ats)]
                for total, at, was, value in zip(sums, ats, held, values[r : r + 4]):
                    total[at, :] = was + value
        return after

    lax.fori_loop(0, senders, add, scale_of(0), unroll=2)

    copies = []
    width = count // sent.shape[0]
    for part in range(sent.shape[0]):

        def finish(i, _):
            at = pl.ds(pl.multiple_of(i * 128, 128), 128)
            total = (sums[0][at, :] + sums[1][at, :]) + (sums[2][at, :] + sums[3][at, :])
            made[:, at] = total.T * jnp.exp(param[pl.ds(i, 1), :])
            return 0

        lax.fori_loop(part * width // 128, (part + 1) * width // 128, finish, 0, unroll=4)
        at = pl.ds(part * width, width)
        copies.append(pltpu.make_async_copy(made.at[:, at], out.at[:, at], sent.at[part]))
        copies[-1].start()
    for copy in copies:
        copy.wait()


def whole(shape):
    zeros = (0,) * len(shape)
    return pl.BlockSpec(shape, lambda *_: zeros)


def on_device(fields, strain_map, quad_weight, param, elem_order, send_elem, send_count, recv_cell):
    planes = jnp.transpose(fields, (0, 2, 1, 3))
    face = jnp.transpose(shifted(fields[0:1], "slab"), (0, 2, 1, 3))[0]
    corner = shifted_both(fields[0:1, 0:1])[0, 0]
    side = shifted(fields[:, 0:1], "cross")[:, 0]
    q_rows, k_cols, perm, basis = tables()
    elems = elem_order.shape[0]
    smem = pl.BlockSpec(memory_space=pltpu.SMEM)
    vmem = pl.BlockSpec(memory_space=pltpu.VMEM)
    params = pltpu.CompilerParams(vmem_limit_bytes=VMEM_BYTES)

    placed, slots, places = pl.pallas_call(
        prepare_kernel,
        out_shape=(
            jax.ShapeDtypeStruct((elems // 128, 32, 128), F32),
            jax.ShapeDtypeStruct((HALF, 128), I32),
            jax.ShapeDtypeStruct((HALF, 128), I32),
        ),
        in_specs=[smem] + [vmem] * 5,
        out_specs=(vmem, vmem, vmem),
        scratch_shapes=[pltpu.VMEM((elems, 32), F32), pltpu.VMEM((elems, 32), F32)],
        compiler_params=params,
    )(elem_order, quad_weight, elem_order.reshape(elems // 128, 128), send_elem[0].T, send_count, recv_cell[0].T)

    block = (1, 257, 8, 128)
    side_block = (1, 257, 128)
    odd = lambda s: jnp.maximum(2 * s - 1, 1)
    even = lambda s: jnp.minimum(2 * s, 14)
    words = pl.pallas_call(
        partial_kernel,
        grid=(9,),
        out_shape=jax.ShapeDtypeStruct((128 * 33, 128), I32),
        in_specs=[
            smem,
            pl.BlockSpec(block, lambda s: (odd(s), 0, 0, 0)),
            pl.BlockSpec(block, lambda s: (even(s), 0, 0, 0)),
            pl.BlockSpec(side_block, lambda s: (odd(s), 0, 0)),
            pl.BlockSpec(side_block, lambda s: (even(s), 0, 0)),
            whole((257, 8, 128)),
            whole((257, 128)),
            whole(placed.shape),
            whole(strain_map.shape),
            whole(q_rows.shape),
            whole(k_cols.shape),
            whole(perm.shape),
            whole(basis.shape),
        ],
        out_specs=whole((128 * 33, 128)),
        scratch_shapes=[
            pltpu.VMEM((2, 2 * ODD_FROM, 128), F32),
            pltpu.VMEM((2, 264, 128), F32),
            pltpu.VMEM((3, 32, 160, 128), BF16),
            pltpu.VMEM((ROWS_Q, 3 * ROWS_K), BF16),
            pltpu.VMEM((512, 512), BF16),
            pltpu.VMEM((512, 512), BF16),
            pltpu.VMEM((elems, 128), F32),
            pltpu.VMEM((elems + 8, 128), I32),
            pltpu.VMEM((elems + 8, 128), I32),
        ],
        compiler_params=params,
    )(slots, planes, planes, side, side, face, corner, placed, strain_map, q_rows, k_cols, perm, basis)

    arrived = lax.all_to_all(words.reshape(128, 33, 1, 128), AXES, split_axis=0, concat_axis=0, tiled=True)
    cells = param.shape[0]
    terms = pl.pallas_call(
        collect_kernel,
        out_shape=jax.ShapeDtypeStruct((128, cells), F32),
        in_specs=[smem, vmem, vmem],
        out_specs=pl.BlockSpec(memory_space=pl.ANY),
        scratch_shapes=[pltpu.VMEM((128, cells), F32), pltpu.SemaphoreType.DMA((8,))]
        + [pltpu.VMEM((cells, 128), F32)] * 4,
        compiler_params=params,
    )(places, arrived.reshape(128 * 33, 128), param.reshape(cells // 128, 128))
    return terms.reshape(16, 8, cells)


def solution(mesh):
    return jax.shard_map(
        on_device,
        mesh=mesh,
        in_specs=(
            P("slab", "cross", None, None),
            P(),
            P(None, AXES),
            P(AXES),
            P(AXES),
            P(AXES, None, None),
            P(AXES, None),
            P(AXES, None, None),
        ),
        out_specs=P(None, None, AXES),
        check_vma=False,
    )
```
